256 devices in a mesh: oct: 8 (over x, core), box: 32 (over y, z).
Axes of the slice: x: 4, y: 4, z: 8, core: 2. Of those that a mesh axis runs over, the one named last changes fastest.
Arguments:
- multipole6: float32 [121, 32768], P(None, ('oct', 'box')), may hold values from -21 to 21
- local5: float32 [121, 4096], P(None, ('oct', 'box')), may hold values from -6 to 6
- box_ids: int32 [4096], P(('oct', 'box')), may hold values from 0 to 32767, as said below
- box_count: int32 [256], P(('oct', 'box')), may hold values from 1 to 16, as said below
- up_shift: float32 [8, 121, 121], replicated, may hold values from -0.5 to 0.5
- down_shift: float32 [8, 121, 121], replicated, may hold values from -0.5 to 0.5
- periodic_lattice_operator: float32 [121, 121], replicated, may hold values from -0.0029296875 to 0.0029296875
- multipole_to_wave_maps: float32 [6, 256, 121], replicated, may hold values from -0.5 to 0.5
- wave_to_local_maps: float32 [6, 121, 256], replicated, may hold values from -0.0625 to 0.0625
- wave_shift: float32 [6, 36, 256], replicated, may hold values from 0.02 to 1
- local_source: int32 [6, 256, 2048], P(None, ('oct', 'box')), may hold values from 0 to 127, as said below
- local_target: int32 [6, 256, 2048], P(None, ('oct', 'box')), may hold values from 0 to 127, as said below
- local_class: int32 [6, 256, 2048], P(None, ('oct', 'box')), may hold values from 0 to 35
- remote_source: int32 [6, 256, 8, 64], P(None, ('oct', 'box')), may hold values from 0 to 127, as said below
- remote_class: int32 [6, 256, 8, 64], P(None, ('oct', 'box')), may hold values from 0 to 35
- remote_count: int32 [6, 256, 8], P(None, ('oct', 'box')), may hold values from 0 to 64, as said below
- arrival_slot: int32 [6, 256, 8, 64], P(None, ('oct', 'box')), may hold values from 0 to 127, as said below
Outputs:
- local6: float32 [121, 32768], P(None, ('oct', 'box'))
The draws below stay inside these ranges and needn't reach their ends.
Inputs may be any that keep to these rules, and one draw needn't show every extreme that they name: `box_count`: 16 is reached by some device in every draw. `box_ids`: device q holds consecutive Morton ids in its slots, starting at q * 128 plus an offset, in slots below its count; slots beyond hold 0; the first device starts at 0 and the last device's range ends at the last id. `local_source`: a slot of a box that device q holds, below 8 box_count[q]. `local_target`: a slot of a box that device q holds, below 8 box_count[q]; every entry is valid. `remote_source`: a slot of a box that the sender holds, below 8 times its count. `remote_count`: in each direction some receiver gets exactly 64 entries from each of its 8 neighbours. `arrival_slot`: a slot of a box that the receiver holds, below 8 times its count; entries at or past the count carry nothing.
All inputs are finite; a program needn't handle non-finite values.
Results may differ from the reference program's by a relative error of at most 0.0003.
Values sent between devices are 32-bit elements; how exact they have to be, the bound alone decides.
A program may use at most 128 MiB of HBM per device.

```python
import math
import jax
import jax.numpy as jnp
from jax import lax

K = 121
NEXP = 256
CLASSES = 36
DEPTH = 5
NEIGH = 8
BOX5 = 16
CAP = 64
LOC = 2048
SLOTS = 128
RANGE5 = 128
PEERS = 256
BOXES5 = 4096
BOXES6 = 32768
N_OCT = 8
N_BOX = 32


def device_counts(key):
    devices = BOXES5 // BOX5
    first_key, second_key = jax.random.split(key)
    counts = jax.random.randint(first_key, (devices,), max(1, BOX5 // 4), BOX5 + 1, dtype=jnp.int32)
    fullest = jax.random.randint(second_key, (), 0, devices, dtype=jnp.int32)
    return jnp.where(jnp.arange(devices, dtype=jnp.int32) == fullest, BOX5, counts)


def draw_box_count(key, part):
    return device_counts(key)


def draw_box_ids(key, part):
    counts = device_counts(key)
    key = jax.random.fold_in(key, 3)
    devices = BOXES5 // BOX5
    device_index = jnp.arange(devices, dtype=jnp.int32)
    offsets = jax.random.randint(key, (devices,), 0, RANGE5 - counts + 1, dtype=jnp.int32)
    offsets = jnp.where(device_index == devices - 1, RANGE5 - counts, offsets)
    offsets = jnp.where(device_index == 0, 0, offsets)
    starts = device_index * RANGE5 + offsets
    slot_index = jnp.arange(BOX5, dtype=jnp.int32)
    numbers = jnp.where(slot_index[None, :] < counts[:, None], starts[:, None] + slot_index[None, :], 0)
    return numbers.reshape(-1).astype(jnp.int32)


def draw_local_source(key, part):
    counts = device_counts(key)
    key = jax.random.fold_in(key, 5)
    devices = BOXES5 // BOX5
    return jax.random.randint(key, (6, devices, LOC), 0, 8 * counts[None, :, None], dtype=jnp.int32)


def draw_local_target(key, part):
    counts = device_counts(key)
    key = jax.random.fold_in(key, 7)
    devices = BOXES5 // BOX5
    return jax.random.randint(key, (6, devices, LOC), 0, 8 * counts[None, :, None], dtype=jnp.int32)


def draw_remote_source(key, part):
    counts = device_counts(key)
    key = jax.random.fold_in(key, 9)
    devices = BOXES5 // BOX5
    return jax.random.randint(key, (6, devices, NEIGH, CAP), 0, 8 * counts[None, :, None, None], dtype=jnp.int32)


def draw_arrival_slot(key, part):
    counts = device_counts(key)
    key = jax.random.fold_in(key, 13)
    devices = BOXES5 // BOX5
    return jax.random.randint(key, (6, devices, NEIGH, CAP), 0, 8 * counts[None, :, None, None], dtype=jnp.int32)


def draw_remote_count(key, part):
    key = jax.random.fold_in(key, 17)
    devices = BOXES5 // BOX5
    first_key, second_key = jax.random.split(key)
    counts = jax.random.randint(first_key, (6, devices, NEIGH), 0, CAP + 1, dtype=jnp.int32)
    fullest = jax.random.randint(second_key, (6,), 0, devices, dtype=jnp.int32)
    neighbour_index = jnp.arange(NEIGH, dtype=jnp.int32)
    offsets = (neighbour_index // 2 + 1) * (1 - 2 * (neighbour_index % 2))
    device_index = jnp.arange(devices, dtype=jnp.int32)
    receivers = (device_index[:, None] + offsets[None, :]) % devices
    return jnp.where(receivers[None, :, :] == fullest[:, None, None], CAP, counts).astype(jnp.int32)


def draw_multipole6(key, part):
    key = jax.random.fold_in(key, 19)
    devices = BOXES6 // SLOTS
    device_of = (jnp.arange(BOXES6, dtype=jnp.int32) // SLOTS).astype(jnp.float32)
    column_scale = 1.0 + 2.0 * device_of / max(devices - 1, 1)
    first_key = jax.random.fold_in(key, 0)
    values = jax.random.truncated_normal(first_key, -4.0, 4.0, (K, BOXES6), jnp.float32)
    return (values * column_scale[None, :]).astype(jnp.float32)


def touch_ends(values, stream_key, smallest, largest):
    index_at = [jax.random.randint(jax.random.fold_in(stream_key, axis), (), 0, length) for axis, length in enumerate(values.shape)]
    longest = values.shape.index(max(values.shape))
    next_to = index_at[:longest] + [(index_at[longest] + 1) % values.shape[longest]] + index_at[longest + 1:]
    return values.at[tuple(index_at)].set(smallest).at[tuple(next_to)].set(largest)


def shard_levels(rng, dims, shards, smallest, top_value):
    gain, own = 1.0, jax.random.fold_in(rng, 6)
    for axis_at, blocks in shards:
        draws = jnp.exp(jax.random.uniform(jax.random.fold_in(own, axis_at), (blocks,), jnp.float32, smallest / len(shards), top_value / len(shards)))
        gain = gain * jnp.repeat(draws, dims[axis_at] // blocks).reshape([-1 if axis == axis_at else 1 for axis in range(len(dims))])
    return gain


def normal_values(key, shape, spread, reach, cuts=(), kind=jnp.bfloat16):
    entries = spread * jax.random.normal(key, shape, jnp.float32)
    if cuts:
        entries = entries * shard_levels(key, shape, cuts, -0.22, 0.18)
    return jnp.clip(entries, -reach, reach).astype(kind)


def setup_inputs(seed: int = 0) -> dict:
    splits = jax.random.split(jax.random.key(seed), 18)
    return {
        "multipole6": draw_multipole6(jax.random.fold_in(splits[17], 71), 0),
        "local5": normal_values(splits[1], (K, BOXES5), 1.0, 6.0, ((1, 256),), jnp.float32),
        "box_ids": draw_box_ids(jax.random.fold_in(splits[17], 71), 0),
        "box_count": draw_box_count(jax.random.fold_in(splits[17], 71), 0),
        "up_shift": normal_values(splits[4], (8, K, K), K ** -0.5, 0.5, (), jnp.float32),
        "down_shift": normal_values(splits[5], (8, K, K), K ** -0.5, 0.5, (), jnp.float32),
        "periodic_lattice_operator": normal_values(splits[6], (K, K), (8 * K * BOXES5) ** -0.5, 0.0029296875, (), jnp.float32),
        "multipole_to_wave_maps": normal_values(splits[7], (6, NEXP, K), K ** -0.5, 0.5, (), jnp.float32),
        "wave_to_local_maps": normal_values(splits[8], (6, K, NEXP), (32 * NEXP) ** -0.5, 0.0625, (), jnp.float32),
        "wave_shift": jnp.clip(jnp.exp(jax.random.uniform(splits[9], (6, CLASSES, NEXP), jnp.float32, math.log(0.02), math.log(1.0))), 0.02, 1.0),
        "local_source": draw_local_source(jax.random.fold_in(splits[17], 71), 0),
        "local_target": draw_local_target(jax.random.fold_in(splits[17], 71), 0),
        "local_class": touch_ends(jax.random.randint(splits[12], (6, PEERS, LOC), 0, CLASSES), jax.random.fold_in(splits[12], 1), 0, CLASSES - 1).astype(jnp.int32),
        "remote_source": draw_remote_source(jax.random.fold_in(splits[17], 71), 0),
        "remote_class": touch_ends(jax.random.randint(splits[14], (6, PEERS, NEIGH, CAP), 0, CLASSES), jax.random.fold_in(splits[14], 1), 0, CLASSES - 1).astype(jnp.int32),
        "remote_count": draw_remote_count(jax.random.fold_in(splits[17], 71), 0),
        "arrival_slot": draw_arrival_slot(jax.random.fold_in(splits[17], 71), 0),
    }


maximal_precision_mode = lax.Precision.HIGHEST


def pick_child(operators, fields, digits):
    translated = jnp.einsum('ckl,lb->ckb', operators, fields, precision=maximal_precision_mode)
    choose = (digits[None, :] == jnp.arange(8, dtype=jnp.int32)[:, None]).astype(fields.dtype)
    return jnp.sum(translated * choose[:, None, :], axis=0)


def level_digits(box_ids):
    return [(box_ids // (8 ** (DEPTH - level_index))) % 8 for level_index in range(1, DEPTH + 1)]


def reference(multipole6, local5, box_ids, box_count, up_shift, down_shift, periodic_lattice_operator, multipole_to_wave_maps, wave_to_local_maps, wave_shift, local_source, local_target, local_class, remote_source, remote_class, remote_count, arrival_slot):
    devices = N_OCT * N_BOX
    child_level_index = jnp.arange(BOXES6, dtype=jnp.int32)
    valid6 = ((child_level_index % SLOTS) < 8 * box_count[child_level_index // SLOTS]).astype(jnp.float32)
    coarse_index = jnp.arange(BOXES5, dtype=jnp.int32)
    valid5 = ((coarse_index % BOX5) < box_count[coarse_index // BOX5]).astype(jnp.float32)
    multipole_moments = multipole6 * valid6[None, :]
    parents = jnp.einsum('ckl,lbc->kb', up_shift, multipole_moments.reshape(K, BOXES5, 8), precision=maximal_precision_mode)
    digits = level_digits(box_ids)
    upward = parents
    for level_index in range(DEPTH - 1, -1, -1):
        upward = pick_child(up_shift, upward, digits[level_index])
    root_moment = jnp.sum(upward * valid5[None, :], axis=1)
    lattice_local = jnp.dot(periodic_lattice_operator, root_moment, precision=maximal_precision_mode)
    downward = jnp.broadcast_to(lattice_local[:, None], (K, BOXES5))
    for level_index in range(DEPTH):
        downward = pick_child(down_shift, downward, digits[level_index])
    coarse = local5 + downward
    result = jnp.einsum('ckl,lb->kbc', down_shift, coarse, precision=maximal_precision_mode).reshape(K, BOXES6)
    entry_index = jnp.arange(CAP, dtype=jnp.int32)
    device_index = jnp.arange(devices, dtype=jnp.int32)
    neighbour_index = jnp.arange(NEIGH, dtype=jnp.int32)
    offsets = (neighbour_index // 2 + 1) * (1 - 2 * (neighbour_index % 2))
    receivers = ((device_index[:, None] + offsets[None, :]) % devices).astype(jnp.int32)
    for direction in range(6):
        local_expansions = jnp.dot(multipole_moments.T, multipole_to_wave_maps[direction].T, precision=maximal_precision_mode)
        factors = wave_shift[direction]
        arrival_by_sender = arrival_slot[direction][receivers, neighbour_index[None, :]]

        def one_device(wave_sums, inputs):
            source_device, near_source, near_target, near_class, far_source, far_class, far_count, far_target, far_receivers = inputs
            offset = source_device * SLOTS
            near_rows = local_expansions[offset + near_source] * factors[near_class]
            wave_sums = wave_sums.at[offset + near_target].add(near_rows)
            weight = (entry_index[None, :] < far_count[:, None]).astype(wave_sums.dtype)
            far_rows = local_expansions[offset + far_source] * factors[far_class] * weight[:, :, None]
            targets = far_receivers[:, None] * SLOTS + far_target
            wave_sums = wave_sums.at[targets.reshape(-1)].add(far_rows.reshape(-1, NEXP))
            return wave_sums, None

        wave_sums, _unused = lax.scan(one_device, jnp.zeros((BOXES6, NEXP), jnp.float32), (device_index, local_source[direction], local_target[direction], local_class[direction], remote_source[direction], remote_class[direction], remote_count[direction], arrival_by_sender, receivers))
        result = result + jnp.dot(wave_to_local_maps[direction], wave_sums.T, precision=maximal_precision_mode)
    return result * valid6[None, :]
```

```python
import functools

import jax
import jax.numpy as jnp
from jax import lax
from jax.experimental import pallas as pl
from jax.experimental.pallas import tpu as pltpu
from jax.sharding import PartitionSpec as P

K = 121
KP = 128
NEXP = 256
CLASSES = 36
DEPTH = 5
NEIGH = 8
BOX5 = 16
CAP = 64
LOC = 2048
SLOTS = 128
BLOCKS = LOC // 128
DIRS = 6
OFFSETS = [(n // 2 + 1) * (1 if n % 2 == 0 else -1) for n in range(NEIGH)]
MESH = pl.DeviceIdType.MESH
F32 = jnp.float32
BF16 = jnp.bfloat16


def split(x):
    hi = x.astype(BF16)
    return hi, (x - hi.astype(F32)).astype(BF16)


def mm(a, b):
    return jnp.dot(a, b, preferred_element_type=F32)


def mm_nt(a, b):
    return lax.dot_general(a, b, (((1,), (1,)), ((), ())), preferred_element_type=F32)


def mm3(a, b):
    ah, al = split(a)
    bh, bl = split(b)
    return mm(ah, bh) + (mm(ah, bl) + mm(al, bh))


def pick_lanes(table, index):
    index = jnp.broadcast_to(index, table.shape)
    numbers = lax.GatherDimensionNumbers(
        offset_dims=(),
        collapsed_slice_dims=(1,),
        start_index_map=(1,),
        operand_batching_dims=(0,),
        start_indices_batching_dims=(0,),
    )
    return lax.gather(
        table,
        index[..., None],
        numbers,
        slice_sizes=(1, 1),
        mode=lax.GatherScatterMode.PROMISE_IN_BOUNDS,
    )


def lane_iota(rows):
    return lax.broadcasted_iota(jnp.int32, (rows, 128), 1)


def one_hot_rows(index):
    rows = lax.broadcasted_iota(jnp.int32, (128, 128), 0)
    return jnp.where(rows == index, 1.0, 0.0).astype(BF16)


def shift_level(high_ref, low_ref, fields, digits):
    fh, fl = split(fields)
    total = jnp.zeros((KP, 128), F32)
    for c in range(8):
        mask = jnp.where(digits == c, 1.0, 0.0).astype(BF16)
        ch, cl = fh * mask, fl * mask
        total = total + (mm(high_ref[c], ch) + (mm(high_ref[c], cl) + mm(low_ref[c], ch)))
    return total


def scatter_block(rows, target):
    hi, lo = split(rows)
    hot = one_hot_rows(target)
    return mm_nt(jnp.concatenate([hi, lo], axis=1), jnp.concatenate([hot, hot], axis=1))


def kernel(
    comm,
    multipole_ref,
    local5_ref,
    ids_ref,
    count_ref,
    up_ref,
    down_ref,
    lattice_ref,
    to_wave_ref,
    to_local_ref,
    shift_ref,
    near_source_ref,
    near_target_ref,
    near_class_ref,
    far_source_ref,
    far_class_ref,
    far_count_ref,
    arrival_ref,
    out_ref,
    moments,
    far_moments,
    pack,
    far_pack,
    padded,
    up_high,
    up_low,
    down_high,
    down_low,
    expansion,
    factor,
    sums,
    ring_a,
    ring_b,
    far_send,
    far_recv,
    pack_send,
    pack_recv,
    a_send,
    a_recv,
    b_send,
    b_recv,
):
    if comm:
        octant, box = lax.axis_index("oct"), lax.axis_index("box")
        flat = octant * 32 + box
        x, core = lax.div(octant, 2), lax.rem(octant, 2)
        y, z = lax.div(box, 8), lax.rem(box, 8)

        def neighbour(offset):
            other = lax.rem(flat + offset + 256, 256)
            return lax.div(other, 32), lax.rem(other, 32)

        def peer_a(k):
            rank = lax.rem(core * 8 + z + k, 16)
            return x * 2 + lax.div(rank, 8), y * 8 + lax.rem(rank, 8)

        def peer_b(k):
            rank = lax.rem(x * 4 + y + k, 16)
            return lax.div(rank, 4) * 2 + core, lax.rem(rank, 4) * 8 + z

        barrier = pltpu.get_barrier_semaphore()
        for n in range(NEIGH):
            pl.semaphore_signal(barrier, inc=1, device_id=neighbour(OFFSETS[n]), device_id_type=MESH)

        def greet(k, carry):
            pl.semaphore_signal(barrier, inc=1, device_id=peer_a(k), device_id_type=MESH)
            pl.semaphore_signal(barrier, inc=1, device_id=peer_b(k), device_id_type=MESH)
            return carry

        lax.fori_loop(1, 16, greet, 0)

    lanes = lane_iota(1)
    count = count_ref[0]
    valid = jnp.where(lanes < 8 * count, 1.0, 0.0)

    moments[...] = jnp.zeros((KP, 128), F32)
    moments[:K, :] = multipole_ref[...] * valid

    wide_lane = lax.broadcasted_iota(jnp.int32, (NEIGH, CAP), 1)
    row_number = lax.broadcasted_iota(jnp.int32, (NEIGH, CAP), 0)
    for d in range(DIRS):
        limit = jnp.zeros((NEIGH, CAP), jnp.int32)
        for n in range(NEIGH):
            limit = jnp.where(row_number == n, far_count_ref[d, 0, n], limit)
        source = jnp.where(wide_lane < limit, far_source_ref[d], -1)
        pack[:, d, :] = jnp.concatenate([source, far_class_ref[d]], axis=1)

    padded[...] = jnp.zeros((KP, KP), F32)
    for c in range(8):
        padded[:K, :K] = up_ref[:, c, :]
        up_high[c], up_low[c] = split(padded[...])
        padded[:K, :K] = down_ref[:, c, :]
        down_high[c], down_low[c] = split(padded[...])

    ids = jnp.concatenate([ids_ref[...], jnp.zeros((1, 128 - BOX5), jnp.int32)], axis=1)
    parent_of = lane_iota(8) // 8
    ids = pick_lanes(jnp.broadcast_to(ids, (8, 128)), parent_of[:1])[:1]
    child = lanes % 8
    digit = [(ids >> (3 * (DEPTH - j))) & 7 for j in range(1, DEPTH + 1)]

    upward = shift_level(up_high, up_low, moments[...], child)
    for j in range(DEPTH - 1, -1, -1):
        upward = shift_level(up_high, up_low, upward, digit[j])
    upward = upward * valid
    ring_a[0] = jnp.sum(jnp.transpose(upward), axis=0, keepdims=True)

    if comm:
        pl.semaphore_wait(barrier, NEIGH + 15 + 15)

        def far_copies(n):
            who = neighbour(OFFSETS[n])
            return (
                pltpu.make_async_remote_copy(
                    src_ref=moments,
                    dst_ref=far_moments.at[n],
                    send_sem=far_send.at[n],
                    recv_sem=far_recv.at[n],
                    device_id=who,
                    device_id_type=MESH,
                ),
                pltpu.make_async_remote_copy(
                    src_ref=pack.at[n],
                    dst_ref=far_pack.at[n],
                    send_sem=pack_send.at[n],
                    recv_sem=pack_recv.at[n],
                    device_id=who,
                    device_id_type=MESH,
                ),
            )

        def sum_copy(k, ring, send, recv, peer):
            return pltpu.make_async_remote_copy(
                src_ref=ring.at[0],
                dst_ref=ring.at[k],
                send_sem=send.at[k - 1],
                recv_sem=recv.at[k - 1],
                device_id=peer(k),
                device_id_type=MESH,
            )

        def for_peers(action):
            def body(k, carry):
                action(k)
                return carry

            lax.fori_loop(1, 16, body, 0)

        copy_a = lambda k: sum_copy(k, ring_a, a_send, a_recv, peer_a)
        copy_b = lambda k: sum_copy(k, ring_b, b_send, b_recv, peer_b)
        for_peers(lambda k: copy_a(k).start())
        far = [far_copies(n) for n in range(NEIGH)]
        for pair in far:
            for copy in pair:
                copy.start()
    else:
        for n in range(NEIGH):
            far_moments[n] = moments[...]
            far_pack[n] = pack[n]

    def near_direction(d, carry):
        weight = to_wave_ref[d]
        mh, ml = split(moments[:K, :])
        wh, wl = split(weight)
        expansion[...] = mm(wh, mh) + (mm(wh, ml) + mm(wl, mh))
        table = jnp.concatenate([shift_ref[d], jnp.zeros((128 - CLASSES, NEXP), F32)], axis=0)
        factor[d] = jnp.transpose(table)
        total = jnp.zeros((NEXP, 128), F32)
        for block in range(BLOCKS):
            source = near_source_ref[d, pl.ds(block, 1), :]
            klass = near_class_ref[d, pl.ds(block, 1), :]
            target = near_target_ref[d, pl.ds(block, 1), :]
            rows = pick_lanes(expansion[...], source) * pick_lanes(factor[d], klass)
            total = total + scatter_block(rows, target)
        sums[d] = total
        return carry

    lax.fori_loop(0, DIRS // 2, near_direction, 0)

    if comm:
        for_peers(lambda k: copy_a(k).wait())
        ring_b[0] = jnp.sum(ring_a[...], axis=0)
        for_peers(lambda k: copy_b(k).start())
    else:
        ring_b[0] = ring_a[0]

    lax.fori_loop(DIRS // 2, DIRS, near_direction, 0)

    if comm:
        for_peers(lambda k: copy_b(k).wait())
        root = jnp.sum(ring_b[...], axis=0)
    else:
        root = ring_b[0]

    padded[:K, :K] = lattice_ref[...]
    ah, al = split(padded[...])
    rh, rl = split(jnp.broadcast_to(root, (128, KP)))
    downward = mm_nt(ah, rh) + (mm_nt(ah, rl) + mm_nt(al, rh))
    for j in range(DEPTH):
        downward = shift_level(down_high, down_low, downward, digit[j])
    padded[...] = jnp.zeros((KP, KP), F32)
    padded[:BOX5, :K] = local5_ref[...]
    coarse = pick_lanes(jnp.transpose(padded[...]), parent_of[:1]) + downward
    result = shift_level(down_high, down_low, coarse, child)[:K]

    if comm:
        for pair in far:
            for copy in pair:
                copy.wait()

    first_half = lanes < CAP

    def far_direction(d, result):
        wh, wl = split(to_wave_ref[d])
        total = sums[d]
        arrival = jnp.concatenate([arrival_ref[d], arrival_ref[d]], axis=1)
        for p in range(NEIGH // 2):
            one = far_pack[2 * p, pl.ds(d, 1), :]
            two = far_pack[2 * p + 1, pl.ds(d, 1), :]
            source = jnp.where(first_half, one, pltpu.roll(two, CAP, 1))
            klass = jnp.where(first_half, pltpu.roll(one, CAP, 1), two)
            target = jnp.where(first_half, arrival[2 * p : 2 * p + 1], arrival[2 * p + 1 : 2 * p + 2])
            target = jnp.where(source >= 0, target, -1)
            source = jnp.maximum(source, 0)
            picked = jnp.where(
                first_half,
                pick_lanes(far_moments[2 * p], source),
                pick_lanes(far_moments[2 * p + 1], source),
            )[:K]
            ph, pl_ = split(picked)
            rows = mm(wh, ph) + (mm(wh, pl_) + mm(wl, ph))
            rows = rows * pick_lanes(factor[d], klass)
            total = total + scatter_block(rows, target)
        return result + mm3(to_local_ref[d], total)

    result = lax.fori_loop(0, DIRS, far_direction, result)
    out_ref[...] = result * valid


def local(
    multipole6,
    local5,
    box_ids,
    box_count,
    up_shift,
    down_shift,
    periodic_lattice_operator,
    multipole_to_wave_maps,
    wave_to_local_maps,
    wave_shift,
    local_source,
    local_target,
    local_class,
    remote_source,
    remote_class,
    remote_count,
    arrival_slot,
    comm=True,
):
    vmem = pl.BlockSpec(memory_space=pltpu.VMEM)
    smem = pl.BlockSpec(memory_space=pltpu.SMEM)
    dma = pltpu.SemaphoreType.DMA
    return pl.pallas_call(
        functools.partial(kernel, comm),
        out_shape=jax.ShapeDtypeStruct((K, SLOTS), F32),
        in_specs=[vmem] * 3 + [smem] + [vmem] * 11 + [smem] + [vmem],
        out_specs=vmem,
        scratch_shapes=[
            pltpu.VMEM((KP, 128), F32),
            pltpu.VMEM((NEIGH, KP, 128), F32),
            pltpu.VMEM((NEIGH, 8, 128), jnp.int32),
            pltpu.VMEM((NEIGH, 8, 128), jnp.int32),
            pltpu.VMEM((KP, KP), F32),
            pltpu.VMEM((8, KP, KP), BF16),
            pltpu.VMEM((8, KP, KP), BF16),
            pltpu.VMEM((8, KP, KP), BF16),
            pltpu.VMEM((8, KP, KP), BF16),
            pltpu.VMEM((NEXP, 128), F32),
            pltpu.VMEM((DIRS, NEXP, 128), F32),
            pltpu.VMEM((DIRS, NEXP, 128), F32),
            pltpu.VMEM((16, 1, 128), F32),
            pltpu.VMEM((16, 1, 128), F32),
            dma((NEIGH,)),
            dma((NEIGH,)),
            dma((NEIGH,)),
            dma((NEIGH,)),
            dma((15,)),
            dma((15,)),
            dma((15,)),
            dma((15,)),
        ],
        compiler_params=pltpu.CompilerParams(
            vmem_limit_bytes=40 * 1024 * 1024,
            **(dict(collective_id=0, has_side_effects=True) if comm else {}),
        ),
        name="downward_pass",
    )(
        multipole6,
        jnp.transpose(local5),
        box_ids.reshape(1, BOX5),
        box_count,
        jnp.transpose(up_shift, (1, 0, 2)),
        jnp.transpose(down_shift, (1, 0, 2)),
        periodic_lattice_operator,
        multipole_to_wave_maps,
        wave_to_local_maps,
        wave_shift,
        local_source.reshape(DIRS, BLOCKS, 128),
        local_target.reshape(DIRS, BLOCKS, 128),
        local_class.reshape(DIRS, BLOCKS, 128),
        remote_source.reshape(DIRS, NEIGH, CAP),
        remote_class.reshape(DIRS, NEIGH, CAP),
        remote_count,
        arrival_slot.reshape(DIRS, NEIGH, CAP),
    )


def solution(mesh):
    split_axes = ("oct", "box")
    return jax.shard_map(
        local,
        mesh=mesh,
        in_specs=(
            P(None, split_axes),
            P(None, split_axes),
            P(split_axes),
            P(split_axes),
            P(),
            P(),
            P(),
            P(),
            P(),
            P(),
            P(None, split_axes, None),
            P(None, split_axes, None),
            P(None, split_axes, None),
            P(None, split_axes, None, None),
            P(None, split_axes, None, None),
            P(None, split_axes, None),
            P(None, split_axes, None, None),
        ),
        out_specs=P(None, split_axes),
        check_vma=False,
    )
```

```python
import functools

import jax
import jax.numpy as jnp
from jax import lax
from jax.experimental import pallas as pl
from jax.experimental.pallas import tpu as pltpu
from jax.sharding import PartitionSpec as P

K = 121
KP = 128
NEXP = 256
CLASSES = 36
DEPTH = 5
NEIGH = 8
BOX5 = 16
CAP = 64
LOC = 2048
SLOTS = 128
BLOCKS = LOC // 128
DIRS = 6
OFFSETS = [(n // 2 + 1) * (1 if n % 2 == 0 else -1) for n in range(NEIGH)]
MESH = pl.DeviceIdType.MESH
LOADS = (
    "multipole",
    "local5",
    "ids",
    "count",
    "up",
    "down",
    "lattice",
    "to_wave",
    "to_local",
    "shift",
    "near_source",
    "near_target",
    "near_class",
    "far_source",
    "far_class",
    "far_count",
    "arrival",
)
LOAD_ORDER = (
    "count",
    "far_count",
    "ids",
    "multipole",
    "far_source",
    "far_class",
    "up",
    "to_wave",
    "shift",
    "near_source",
    "near_class",
    "near_target",
    "down",
    "lattice",
    "local5",
    "arrival",
    "to_local",
)
F32 = jnp.float32
BF16 = jnp.bfloat16


def split(x):
    hi = x.astype(BF16)
    return hi, (x - hi.astype(F32)).astype(BF16)


def mm(a, b):
    return jnp.dot(a, b, preferred_element_type=F32)


def mm_nt(a, b):
    return lax.dot_general(a, b, (((1,), (1,)), ((), ())), preferred_element_type=F32)


def mm3(a, b):
    ah, al = split(a)
    bh, bl = split(b)
    return mm(ah, bh) + (mm(ah, bl) + mm(al, bh))


def pick_lanes(table, index):
    index = jnp.broadcast_to(index, table.shape)
    numbers = lax.GatherDimensionNumbers(
        offset_dims=(),
        collapsed_slice_dims=(1,),
        start_index_map=(1,),
        operand_batching_dims=(0,),
        start_indices_batching_dims=(0,),
    )
    return lax.gather(
        table,
        index[..., None],
        numbers,
        slice_sizes=(1, 1),
        mode=lax.GatherScatterMode.PROMISE_IN_BOUNDS,
    )


def lane_iota(rows):
    return lax.broadcasted_iota(jnp.int32, (rows, 128), 1)


def one_hot_rows(index):
    rows = lax.broadcasted_iota(jnp.int32, (128, 128), 0)
    return jnp.where(rows == index, 1.0, 0.0).astype(BF16)


def shift_level(high_ref, low_ref, fields, digits, operators):
    fh, fl = split(fields)
    total = jnp.zeros((KP, 128), F32)
    for at in range(0, len(operators), 2):
        group = operators[at : at + 2]
        masks = [jnp.where(digits == c, 1.0, 0.0).astype(BF16) for c in group]
        high = jnp.concatenate([high_ref[c] for c in group], axis=1)
        low = jnp.concatenate([low_ref[c] for c in group], axis=1)
        bh = jnp.concatenate([fh * mask for mask in masks], axis=0)
        bl = jnp.concatenate([fl * mask for mask in masks], axis=0)
        both = mm(high, jnp.concatenate([bh, bl], axis=1))
        total = total + (both[:, :128] + (both[:, 128:] + mm(low, bh)))
    return total


def class_factors(table, klass):
    width = klass.shape[1]
    rows = lax.broadcasted_iota(jnp.int32, (128, width), 0)
    return mm(table, jnp.where(rows % 64 == klass, 1.0, 0.0).astype(BF16))


def halves(rows):
    hi, lo = split(rows)
    return jnp.concatenate([hi, lo], axis=1)


def scatter(target, pair):
    hot = one_hot_rows(target)
    return mm_nt(jnp.concatenate([hot, hot], axis=1), pair)


def kernel(comm, *refs):
    given, out_ref, held, rest = refs[:17], refs[17], refs[18:35], refs[35:]
    (
        multipole_ref,
        local5_ref,
        ids_ref,
        count_ref,
        up_ref,
        down_ref,
        lattice_ref,
        to_wave_ref,
        to_local_ref,
        shift_ref,
        near_source_ref,
        near_target_ref,
        near_class_ref,
        far_source_ref,
        far_class_ref,
        far_count_ref,
        arrival_ref,
    ) = held
    (
        load_sem,
        moments,
        far_moments,
        pack,
        far_pack,
        padded,
        up_high,
        up_low,
        down_high,
        down_low,
        expansion,
        wide,
        wave_halves,
        held_rows,
        table_rows,
        factor,
        sums,
        ring_a,
        ring_b,
        far_send,
        far_recv,
        pack_send,
        pack_recv,
        a_send,
        a_recv,
        b_send,
        b_recv,
    ) = rest
    loads = {
        name: pltpu.make_async_copy(
            given[i],
            held[i].at[pl.ds(0, 8 * K)] if name in ("up", "down") else held[i],
            load_sem.at[i],
        )
        for i, name in enumerate(LOADS)
    }
    for name in LOAD_ORDER:
        loads[name].start()

    def loaded(*names):
        for name in names:
            loads[name].wait()

    if comm:
        octant, box = lax.axis_index("oct"), lax.axis_index("box")
        flat = octant * 32 + box
        x, core = lax.div(octant, 2), lax.rem(octant, 2)
        y, z = lax.div(box, 8), lax.rem(box, 8)

        def neighbour(offset):
            other = lax.rem(flat + offset + 256, 256)
            return lax.div(other, 32), lax.rem(other, 32)

        def peer_a(k):
            rank = lax.rem(core * 8 + z + k, 16)
            return x * 2 + lax.div(rank, 8), y * 8 + lax.rem(rank, 8)

        def peer_b(k):
            rank = lax.rem(x * 4 + y + k, 16)
            return lax.div(rank, 4) * 2 + core, lax.rem(rank, 4) * 8 + z

        barrier = pltpu.get_barrier_semaphore()
        for n in range(NEIGH):
            pl.semaphore_signal(barrier, inc=1, device_id=neighbour(OFFSETS[n]), device_id_type=MESH)

        def greet(k, carry):
            pl.semaphore_signal(barrier, inc=1, device_id=peer_a(k), device_id_type=MESH)
            pl.semaphore_signal(barrier, inc=1, device_id=peer_b(k), device_id_type=MESH)
            return carry

        lax.fori_loop(1, 16, greet, 0)

    loaded("count", "multipole")
    lanes = lane_iota(1)
    count = count_ref[0]
    valid = jnp.where(lanes < 8 * count, 1.0, 0.0)

    moments[...] = jnp.zeros((KP, 128), F32)
    moments[:K, :] = multipole_ref[...] * valid

    loaded("far_count", "far_source", "far_class")
    wide_lane = lax.broadcasted_iota(jnp.int32, (NEIGH, CAP), 1)
    row_number = lax.broadcasted_iota(jnp.int32, (NEIGH, CAP), 0)
    for d in range(DIRS):
        limit = jnp.zeros((NEIGH, CAP), jnp.int32)
        for n in range(NEIGH):
            limit = jnp.where(row_number == n, far_count_ref[d, 0, n], limit)
        source = jnp.where(wide_lane < limit, far_source_ref[d], -1)
        pack[:, d, :] = jnp.concatenate([source, far_class_ref[d]], axis=1)

    loaded("up", "down")
    for ref in (up_ref, down_ref):
        ref[8 * K :, :] = jnp.zeros((8 * (KP - K), K), F32)
    padded[...] = jnp.zeros((KP, KP), F32)
    for c in range(8):
        padded[:, :K] = up_ref[pl.ds(c, KP, stride=8), :]
        up_high[c], up_low[c] = split(padded[...])
        padded[:, :K] = down_ref[pl.ds(c, KP, stride=8), :]
        down_high[c], down_low[c] = split(padded[...])

    loaded("ids")
    first = ids_ref[0]
    parent_of = lanes // 8
    child = lanes % 8
    ids = first + parent_of
    digit = [(ids >> (3 * (DEPTH - j))) & 7 for j in range(1, DEPTH + 1)]
    chosen = [
        [((first >> (3 * (DEPTH - j))) + i) & 7 for i in range(2 if j < DEPTH - 1 else 3)]
        for j in range(1, DEPTH)
    ] + [list(range(8))]

    upward = shift_level(up_high, up_low, moments[...], child, range(8))
    for j in range(DEPTH - 1, -1, -1):
        upward = shift_level(up_high, up_low, upward, digit[j], chosen[j])
    upward = upward * valid
    ring_a[0] = jnp.sum(jnp.transpose(upward), axis=0, keepdims=True)

    if comm:
        pl.semaphore_wait(barrier, NEIGH + 15 + 15)

        def far_copies(n):
            who = neighbour(OFFSETS[n])
            return (
                pltpu.make_async_remote_copy(
                    src_ref=moments,
                    dst_ref=far_moments.at[n],
                    send_sem=far_send.at[n],
                    recv_sem=far_recv.at[n],
                    device_id=who,
                    device_id_type=MESH,
                ),
                pltpu.make_async_remote_copy(
                    src_ref=pack.at[n],
                    dst_ref=far_pack.at[n],
                    send_sem=pack_send.at[n],
                    recv_sem=pack_recv.at[n],
                    device_id=who,
                    device_id_type=MESH,
                ),
            )

        def sum_copy(k, ring, send, recv, peer):
            return pltpu.make_async_remote_copy(
                src_ref=ring.at[0],
                dst_ref=ring.at[k],
                send_sem=send.at[k - 1],
                recv_sem=recv.at[k - 1],
                device_id=peer(k),
                device_id_type=MESH,
            )

        def for_peers(action):
            def body(k, carry):
                action(k)
                return carry

            lax.fori_loop(1, 16, body, 0)

        copy_a = lambda k: sum_copy(k, ring_a, a_send, a_recv, peer_a)
        copy_b = lambda k: sum_copy(k, ring_b, b_send, b_recv, peer_b)
        for_peers(lambda k: copy_a(k).start())
        far = [far_copies(n) for n in range(NEIGH)]
        for pair in far:
            for copy in pair:
                copy.start()
    else:
        for n in range(NEIGH):
            far_moments[n] = moments[...]
            far_pack[n] = pack[n]

    loaded("to_wave", "shift", "near_source", "near_class", "near_target")
    table_rows[...] = jnp.zeros((128, NEXP), F32)
    wide[...] = jnp.zeros((NEXP, KP), F32)
    mh, ml = split(moments[...])
    for d in range(DIRS):
        wide[:, :K] = to_wave_ref[d]
        wh, wl = split(wide[...])
        wave_halves[d] = jnp.concatenate([wh, wl], axis=1)
        both = mm(wh, jnp.concatenate([mh, ml], axis=1))
        expansion[d] = both[:, :128] + (both[:, 128:] + mm(wl, mh))
        high, low = split(shift_ref[d])
        table_rows[:CLASSES, :] = high.astype(F32)
        table_rows[64 : 64 + CLASSES, :] = low.astype(F32)
        factor[d] = jnp.transpose(table_rows[...]).astype(BF16)

    def near_rows(d, block):
        klass = [near_class_ref[d, pl.ds(block + i, 1), :] for i in range(2)]
        factors = class_factors(factor[d], jnp.concatenate(klass, axis=1))
        for i in range(2):
            source = near_source_ref[d, pl.ds(block + i, 1), :]
            rows = pick_lanes(expansion[d], source) * factors[:, 128 * i : 128 * (i + 1)]
            held_rows[block + i] = halves(rows)

    def near_sums(d, block):
        return scatter(near_target_ref[d, pl.ds(block, 1), :], held_rows[block]) + scatter(
            near_target_ref[d, pl.ds(block + 1, 1), :], held_rows[block + 1]
        )

    def near_step(d, carry):
        total = jnp.zeros((128, NEXP), F32)
        for block in range(0, BLOCKS, 2):
            total = total + near_sums(d - 1, block)
            near_rows(d, block)
        sums[d - 1] = total
        return carry

    for block in range(0, BLOCKS, 2):
        near_rows(0, block)

    lax.fori_loop(1, 3, near_step, 0)

    if comm:
        for_peers(lambda k: copy_a(k).wait())
        ring_b[0] = jnp.sum(ring_a[...], axis=0)
        for_peers(lambda k: copy_b(k).start())
    else:
        ring_b[0] = ring_a[0]

    lax.fori_loop(3, 5, near_step, 0)

    if comm:
        for_peers(lambda k: copy_b(k).wait())
        root = jnp.sum(ring_b[...], axis=0)
    else:
        root = ring_b[0]

    near_step(DIRS - 1, 0)
    total = jnp.zeros((128, NEXP), F32)
    for block in range(0, BLOCKS, 2):
        total = total + near_sums(DIRS - 1, block)
    sums[DIRS - 1] = total

    loaded("lattice", "local5", "arrival", "to_local")
    padded[:K, :K] = lattice_ref[...]
    ah, al = split(padded[...])
    rh, rl = split(jnp.broadcast_to(root, (128, KP)))
    downward = mm_nt(ah, rh) + (mm_nt(ah, rl) + mm_nt(al, rh))
    for j in range(DEPTH):
        downward = shift_level(down_high, down_low, downward, digit[j], chosen[j])
    padded[...] = jnp.zeros((KP, KP), F32)
    padded[:BOX5, :K] = local5_ref[...]
    coarse = pick_lanes(jnp.transpose(padded[...]), parent_of) + downward
    result = shift_level(down_high, down_low, coarse, child, range(8))[:K]

    first_half = lanes < CAP

    def far_blocks(group):
        for d in range(DIRS):
            sources, klasses, targets, picked = [], [], [], []
            arrival = jnp.concatenate([arrival_ref[d], arrival_ref[d]], axis=1)
            for p in (2 * group, 2 * group + 1):
                one = far_pack[2 * p, d : d + 1, :]
                two = far_pack[2 * p + 1, d : d + 1, :]
                source = jnp.where(first_half, one, pltpu.roll(two, CAP, 1))
                klasses.append(jnp.where(first_half, pltpu.roll(one, CAP, 1), two))
                target = jnp.where(
                    first_half, arrival[2 * p : 2 * p + 1], arrival[2 * p + 1 : 2 * p + 2]
                )
                targets.append(jnp.where(source >= 0, target, -1))
                source = jnp.maximum(source, 0)
                picked.append(
                    jnp.where(
                        first_half,
                        pick_lanes(far_moments[2 * p], source),
                        pick_lanes(far_moments[2 * p + 1], source),
                    )
                )
            ph, pl_ = split(jnp.concatenate(picked, axis=1))
            both = wave_halves[d]
            rows = mm(both, jnp.concatenate([ph, ph], axis=0)) + mm(both[:, :KP], pl_)
            rows = rows * class_factors(factor[d], jnp.concatenate(klasses, axis=1))
            total = sums[d]
            for i in range(2):
                total = total + scatter(targets[i], halves(rows[:, 128 * i : 128 * (i + 1)]))
            sums[d] = total

    for group in range(2):
        if comm:
            for n in range(4 * group, 4 * group + 4):
                for copy in far[n]:
                    copy.wait()
        far_blocks(group)

    for d in range(DIRS):
        vh, vl = split(to_local_ref[d])
        th, tl = split(sums[d])
        both = mm_nt(vh, jnp.concatenate([th, tl], axis=0))
        result = result + (both[:, :128] + (both[:, 128:] + mm_nt(vl, th)))
    out_ref[...] = result * valid


def local(
    multipole6,
    local5,
    box_ids,
    box_count,
    up_shift,
    down_shift,
    periodic_lattice_operator,
    multipole_to_wave_maps,
    wave_to_local_maps,
    wave_shift,
    local_source,
    local_target,
    local_class,
    remote_source,
    remote_class,
    remote_count,
    arrival_slot,
    comm=True,
):
    dma = pltpu.SemaphoreType.DMA
    operands = (
        multipole6,
        jnp.transpose(local5),
        box_ids,
        box_count,
        jnp.transpose(up_shift, (1, 0, 2)).reshape(8 * K, K),
        jnp.transpose(down_shift, (1, 0, 2)).reshape(8 * K, K),
        periodic_lattice_operator,
        multipole_to_wave_maps,
        wave_to_local_maps,
        wave_shift,
        local_source.reshape(DIRS, BLOCKS, 128),
        local_target.reshape(DIRS, BLOCKS, 128),
        local_class.reshape(DIRS, BLOCKS, 128),
        remote_source.reshape(DIRS, NEIGH, CAP),
        remote_class.reshape(DIRS, NEIGH, CAP),
        remote_count,
        arrival_slot.reshape(DIRS, NEIGH, CAP),
    )
    held = []
    for name, value in zip(LOADS, operands):
        space = pltpu.SMEM if name in ("ids", "count", "far_count") else pltpu.VMEM
        shape = (8 * KP, K) if name in ("up", "down") else value.shape
        held.append(space(shape, value.dtype))
    return pl.pallas_call(
        functools.partial(kernel, comm),
        out_shape=jax.ShapeDtypeStruct((K, SLOTS), F32),
        in_specs=[pl.BlockSpec(memory_space=pltpu.HBM)] * len(operands),
        out_specs=pl.BlockSpec(memory_space=pltpu.VMEM),
        scratch_shapes=held + [
            dma((len(operands),)),
            pltpu.VMEM((KP, 128), F32),
            pltpu.VMEM((NEIGH, KP, 128), F32),
            pltpu.VMEM((NEIGH, 8, 128), jnp.int32),
            pltpu.VMEM((NEIGH, 8, 128), jnp.int32),
            pltpu.VMEM((KP, KP), F32),
            pltpu.VMEM((8, KP, KP), BF16),
            pltpu.VMEM((8, KP, KP), BF16),
            pltpu.VMEM((8, KP, KP), BF16),
            pltpu.VMEM((8, KP, KP), BF16),
            pltpu.VMEM((DIRS, NEXP, 128), F32),
            pltpu.VMEM((NEXP, KP), F32),
            pltpu.VMEM((DIRS, NEXP, 2 * KP), BF16),
            pltpu.VMEM((BLOCKS, NEXP, 256), BF16),
            pltpu.VMEM((128, NEXP), F32),
            pltpu.VMEM((DIRS, NEXP, 128), BF16),
            pltpu.VMEM((DIRS, 128, NEXP), F32),
            pltpu.VMEM((16, 1, 128), F32),
            pltpu.VMEM((16, 1, 128), F32),
            dma((NEIGH,)),
            dma((NEIGH,)),
            dma((NEIGH,)),
            dma((NEIGH,)),
            dma((15,)),
            dma((15,)),
            dma((15,)),
            dma((15,)),
        ],
        compiler_params=pltpu.CompilerParams(
            vmem_limit_bytes=60 * 1024 * 1024,
            **(dict(collective_id=0, has_side_effects=True) if comm else {}),
        ),
        name="downward_pass",
    )(*operands)


def solution(mesh):
    split_axes = ("oct", "box")
    return jax.shard_map(
        local,
        mesh=mesh,
        in_specs=(
            P(None, split_axes),
            P(None, split_axes),
            P(split_axes),
            P(split_axes),
            P(),
            P(),
            P(),
            P(),
            P(),
            P(),
            P(None, split_axes, None),
            P(None, split_axes, None),
            P(None, split_axes, None),
            P(None, split_axes, None, None),
            P(None, split_axes, None, None),
            P(None, split_axes, None),
            P(None, split_axes, None, None),
        ),
        out_specs=P(None, split_axes),
        check_vma=False,
    )
```

```python
import functools

import jax
import jax.numpy as jnp
from jax import lax
from jax.experimental import pallas as pl
from jax.experimental.pallas import tpu as pltpu
from jax.sharding import PartitionSpec as P

K = 121
KP = 128
NEXP = 256
CLASSES = 36
DEPTH = 5
NEIGH = 8
BOX5 = 16
CAP = 64
LOC = 2048
SLOTS = 128
BLOCKS = LOC // 128
DIRS = 6
OFFSETS = [(n // 2 + 1) * (1 if n % 2 == 0 else -1) for n in range(NEIGH)]
MESH = pl.DeviceIdType.MESH
LOADS = (
    "multipole",
    "local5",
    "ids",
    "count",
    "up",
    "down",
    "lattice",
    "to_wave",
    "to_local",
    "shift",
    "near_source",
    "near_target",
    "near_class",
    "far_source",
    "far_class",
    "far_count",
    "arrival",
)
LOAD_ORDER = (
    "count",
    "far_count",
    "ids",
    "multipole",
    "far_source",
    "far_class",
    "up",
    "to_wave",
    "shift",
    "near_source",
    "near_class",
    "near_target",
    "down",
    "lattice",
    "local5",
    "arrival",
    "to_local",
)
F32 = jnp.float32
BF16 = jnp.bfloat16


def split(x):
    hi = x.astype(BF16)
    return hi, (x - hi.astype(F32)).astype(BF16)


def mm(a, b):
    return jnp.dot(a, b, preferred_element_type=F32)


def mm_nt(a, b):
    return lax.dot_general(a, b, (((1,), (1,)), ((), ())), preferred_element_type=F32)


def mm3(a, b):
    ah, al = split(a)
    bh, bl = split(b)
    return mm(ah, bh) + (mm(ah, bl) + mm(al, bh))


def pick_lanes(table, index):
    index = jnp.broadcast_to(index, table.shape)
    numbers = lax.GatherDimensionNumbers(
        offset_dims=(),
        collapsed_slice_dims=(1,),
        start_index_map=(1,),
        operand_batching_dims=(0,),
        start_indices_batching_dims=(0,),
    )
    return lax.gather(
        table,
        index[..., None],
        numbers,
        slice_sizes=(1, 1),
        mode=lax.GatherScatterMode.PROMISE_IN_BOUNDS,
    )


def lane_iota(rows):
    return lax.broadcasted_iota(jnp.int32, (rows, 128), 1)


def one_hot_rows(index):
    rows = lax.broadcasted_iota(jnp.int32, (128, 128), 0)
    return jnp.where(rows == index, 1.0, 0.0).astype(BF16)


def shift_level(high_ref, low_ref, fields, digits, operators):
    fh, fl = split(fields)
    total = jnp.zeros((KP, 128), F32)
    for at in range(0, len(operators), 2):
        group = operators[at : at + 2]
        masks = [jnp.where(digits == c, 1.0, 0.0).astype(BF16) for c in group]
        high = jnp.concatenate([high_ref[c] for c in group], axis=1)
        low = jnp.concatenate([low_ref[c] for c in group], axis=1)
        bh = jnp.concatenate([fh * mask for mask in masks], axis=0)
        bl = jnp.concatenate([fl * mask for mask in masks], axis=0)
        both = mm(high, jnp.concatenate([bh, bl], axis=1))
        total = total + (both[:, :128] + (both[:, 128:] + mm(low, bh)))
    return total


def class_factors(table, klass):
    width = klass.shape[1]
    rows = lax.broadcasted_iota(jnp.int32, (128, width), 0)
    return mm(table, jnp.where(rows % 64 == klass, 1.0, 0.0).astype(BF16))


def halves(rows):
    hi, lo = split(rows)
    return jnp.concatenate([hi, lo], axis=1)


def scatter(target, pair):
    hot = one_hot_rows(target)
    return mm_nt(jnp.concatenate([hot, hot], axis=1), pair)


def kernel(comm, *refs):
    given, out_ref, held, rest = refs[:17], refs[17], refs[18:35], refs[35:]
    (
        multipole_ref,
        local5_ref,
        ids_ref,
        count_ref,
        up_ref,
        down_ref,
        lattice_ref,
        to_wave_ref,
        to_local_ref,
        shift_ref,
        near_source_ref,
        near_target_ref,
        near_class_ref,
        far_source_ref,
        far_class_ref,
        far_count_ref,
        arrival_ref,
    ) = held
    (
        load_sem,
        moments,
        far_moments,
        pack,
        far_pack,
        padded,
        up_high,
        up_low,
        down_high,
        down_low,
        expansion,
        wide,
        wave_halves,
        held_rows,
        table_rows,
        factor,
        sums,
        ring_a,
        ring_b,
        far_send,
        far_recv,
        pack_send,
        pack_recv,
        a_send,
        a_recv,
        b_send,
        b_recv,
    ) = rest
    loads = {
        name: pltpu.make_async_copy(
            given[i],
            held[i].at[pl.ds(0, 8 * K)] if name in ("up", "down") else held[i],
            load_sem.at[i],
        )
        for i, name in enumerate(LOADS)
    }
    for name in LOAD_ORDER:
        loads[name].start()

    def loaded(*names):
        for name in names:
            loads[name].wait()

    if comm:
        octant, box = lax.axis_index("oct"), lax.axis_index("box")
        flat = octant * 32 + box
        x, core = lax.div(octant, 2), lax.rem(octant, 2)
        y, z = lax.div(box, 8), lax.rem(box, 8)

        def neighbour(offset):
            other = lax.rem(flat + offset + 256, 256)
            return lax.div(other, 32), lax.rem(other, 32)

        def peer_a(k):
            rank = lax.rem(core * 8 + z + k, 16)
            return x * 2 + lax.div(rank, 8), y * 8 + lax.rem(rank, 8)

        def peer_b(k):
            rank = lax.rem(x * 4 + y + k, 16)
            return lax.div(rank, 4) * 2 + core, lax.rem(rank, 4) * 8 + z

        barrier = pltpu.get_barrier_semaphore()
        for n in range(NEIGH):
            pl.semaphore_signal(barrier, inc=1, device_id=neighbour(OFFSETS[n]), device_id_type=MESH)

        def greet(k, carry):
            pl.semaphore_signal(barrier, inc=1, device_id=peer_a(k), device_id_type=MESH)
            pl.semaphore_signal(barrier, inc=1, device_id=peer_b(k), device_id_type=MESH)
            return carry

        lax.fori_loop(1, 16, greet, 0)

    loaded("count", "multipole")
    lanes = lane_iota(1)
    count = count_ref[0]
    valid = jnp.where(lanes < 8 * count, 1.0, 0.0)

    moments[...] = jnp.zeros((KP, 128), F32)
    moments[:K, :] = multipole_ref[...] * valid

    loaded("far_count", "far_source", "far_class")
    wide_lane = lax.broadcasted_iota(jnp.int32, (NEIGH, CAP), 1)
    row_number = lax.broadcasted_iota(jnp.int32, (NEIGH, CAP), 0)
    for d in range(DIRS):
        limit = jnp.zeros((NEIGH, CAP), jnp.int32)
        for n in range(NEIGH):
            limit = jnp.where(row_number == n, far_count_ref[d, 0, n], limit)
        source = jnp.where(wide_lane < limit, far_source_ref[d], -1)
        pack[:, d, :] = jnp.concatenate([source, far_class_ref[d]], axis=1)

    if comm:
        pl.semaphore_wait(barrier, NEIGH + 15 + 15)

        def far_copies(n):
            who = neighbour(OFFSETS[n])
            near_by = who if n < 4 else neighbour(OFFSETS[n - 4])
            return (
                pltpu.make_async_remote_copy(
                    src_ref=moments if n < 4 else far_moments.at[2 + n % 2],
                    dst_ref=far_moments.at[n],
                    send_sem=far_send.at[n],
                    recv_sem=far_recv.at[n],
                    device_id=near_by,
                    device_id_type=MESH,
                ),
                pltpu.make_async_remote_copy(
                    src_ref=pack.at[n],
                    dst_ref=far_pack.at[n],
                    send_sem=pack_send.at[n],
                    recv_sem=pack_recv.at[n],
                    device_id=who,
                    device_id_type=MESH,
                ),
            )

        def sum_copy(k, ring, send, recv, peer):
            return pltpu.make_async_remote_copy(
                src_ref=ring.at[0],
                dst_ref=ring.at[k],
                send_sem=send.at[k - 1],
                recv_sem=recv.at[k - 1],
                device_id=peer(k),
                device_id_type=MESH,
            )

        def for_peers(action):
            def body(k, carry):
                action(k)
                return carry

            lax.fori_loop(1, 16, body, 0)

        copy_a = lambda k: sum_copy(k, ring_a, a_send, a_recv, peer_a)
        copy_b = lambda k: sum_copy(k, ring_b, b_send, b_recv, peer_b)
        far = [far_copies(n) for n in range(NEIGH)]
        for n in range(4):
            far[n][0].start()
        for n in range(NEIGH):
            far[n][1].start()
    else:
        for n in range(NEIGH):
            far_moments[n] = moments[...]
            far_pack[n] = pack[n]

    loaded("up", "down", "ids", "to_wave", "shift", "near_source", "near_class", "near_target")
    for ref in (up_ref, down_ref):
        ref[8 * K :, :] = jnp.zeros((8 * (KP - K), K), F32)
    padded[...] = jnp.zeros((KP, KP), F32)
    for c in range(8):
        padded[:, :K] = up_ref[pl.ds(c, KP, stride=8), :]
        up_high[c], up_low[c] = split(padded[...])
        padded[:, :K] = down_ref[pl.ds(c, KP, stride=8), :]
        down_high[c], down_low[c] = split(padded[...])

    first = ids_ref[0]
    parent_of = lanes // 8
    child = lanes % 8
    ids = first + parent_of
    digit = [(ids >> (3 * (DEPTH - j))) & 7 for j in range(1, DEPTH + 1)]
    chosen = [
        [((first >> (3 * (DEPTH - j))) + i) & 7 for i in range(2 if j < DEPTH - 1 else 3)]
        for j in range(1, DEPTH)
    ] + [list(range(8))]

    upward = shift_level(up_high, up_low, moments[...], child, range(8))
    for j in range(DEPTH - 1, -1, -1):
        upward = shift_level(up_high, up_low, upward, digit[j], chosen[j])
    upward = upward * valid
    ring_a[0] = jnp.sum(jnp.transpose(upward), axis=0, keepdims=True)

    table_rows[...] = jnp.zeros((128, NEXP), F32)
    wide[...] = jnp.zeros((NEXP, KP), F32)
    mh, ml = split(moments[...])
    for d in range(DIRS):
        wide[:, :K] = to_wave_ref[d]
        wh, wl = split(wide[...])
        wave_halves[d] = jnp.concatenate([wh, wl], axis=1)
        both = mm(wh, jnp.concatenate([mh, ml], axis=1))
        expansion[d] = both[:, :128] + (both[:, 128:] + mm(wl, mh))
        high, low = split(shift_ref[d])
        table_rows[:CLASSES, :] = high.astype(F32)
        table_rows[64 : 64 + CLASSES, :] = low.astype(F32)
        factor[d] = jnp.transpose(table_rows[...]).astype(BF16)

    def near_rows(d, block):
        klass = [near_class_ref[d, pl.ds(block + i, 1), :] for i in range(2)]
        factors = class_factors(factor[d], jnp.concatenate(klass, axis=1))
        for i in range(2):
            source = near_source_ref[d, pl.ds(block + i, 1), :]
            rows = pick_lanes(expansion[d], source) * factors[:, 128 * i : 128 * (i + 1)]
            held_rows[block + i] = halves(rows)

    def near_sums(d, block):
        return scatter(near_target_ref[d, pl.ds(block, 1), :], held_rows[block]) + scatter(
            near_target_ref[d, pl.ds(block + 1, 1), :], held_rows[block + 1]
        )

    def near_step(d, carry):
        total = jnp.zeros((128, NEXP), F32)
        for block in range(0, BLOCKS, 2):
            total = total + near_sums(d - 1, block)
            near_rows(d, block)
        sums[d - 1] = total
        return carry

    for block in range(0, BLOCKS, 2):
        near_rows(0, block)

    if comm:
        for_peers(lambda k: copy_a(k).start())

    lax.fori_loop(1, 3, near_step, 0)

    if comm:
        for n in (2, 3):
            far[n][0].wait()
        for n in range(4, NEIGH):
            far[n][0].start()
        for_peers(lambda k: copy_a(k).wait())
        ring_b[0] = jnp.sum(ring_a[...], axis=0)
        for_peers(lambda k: copy_b(k).start())
    else:
        ring_b[0] = ring_a[0]

    lax.fori_loop(3, 5, near_step, 0)

    if comm:
        for_peers(lambda k: copy_b(k).wait())
        root = jnp.sum(ring_b[...], axis=0)
    else:
        root = ring_b[0]

    loaded("lattice", "local5", "arrival", "to_local")
    padded[:K, :K] = lattice_ref[...]
    ah, al = split(padded[...])
    rh, rl = split(jnp.broadcast_to(root, (128, KP)))
    downward = mm_nt(ah, rh) + (mm_nt(ah, rl) + mm_nt(al, rh))
    for j in range(DEPTH):
        downward = shift_level(down_high, down_low, downward, digit[j], chosen[j])
    padded[...] = jnp.zeros((KP, KP), F32)
    padded[:BOX5, :K] = local5_ref[...]
    coarse = pick_lanes(jnp.transpose(padded[...]), parent_of) + downward
    result = shift_level(down_high, down_low, coarse, child, range(8))[:K]

    near_step(DIRS - 1, 0)
    total = jnp.zeros((128, NEXP), F32)
    for block in range(0, BLOCKS, 2):
        total = total + near_sums(DIRS - 1, block)
    sums[DIRS - 1] = total

    first_half = lanes < CAP

    def far_blocks(group):
        for d in range(DIRS):
            sources, klasses, targets, picked = [], [], [], []
            arrival = jnp.concatenate([arrival_ref[d], arrival_ref[d]], axis=1)
            for p in (2 * group, 2 * group + 1):
                one = far_pack[2 * p, d : d + 1, :]
                two = far_pack[2 * p + 1, d : d + 1, :]
                source = jnp.where(first_half, one, pltpu.roll(two, CAP, 1))
                klasses.append(jnp.where(first_half, pltpu.roll(one, CAP, 1), two))
                target = jnp.where(
                    first_half, arrival[2 * p : 2 * p + 1], arrival[2 * p + 1 : 2 * p + 2]
                )
                targets.append(jnp.where(source >= 0, target, -1))
                source = jnp.maximum(source, 0)
                picked.append(
                    jnp.where(
                        first_half,
                        pick_lanes(far_moments[2 * p], source),
                        pick_lanes(far_moments[2 * p + 1], source),
                    )
                )
            ph, pl_ = split(jnp.concatenate(picked, axis=1))
            both = wave_halves[d]
            rows = mm(both, jnp.concatenate([ph, ph], axis=0)) + mm(both[:, :KP], pl_)
            rows = rows * class_factors(factor[d], jnp.concatenate(klasses, axis=1))
            total = sums[d]
            for i in range(2):
                total = total + scatter(targets[i], halves(rows[:, 128 * i : 128 * (i + 1)]))
            sums[d] = total

    for group in range(2):
        if comm:
            for n in range(4 * group, 4 * group + 4):
                if n not in (2, 3):
                    far[n][0].wait()
                far[n][1].wait()
        far_blocks(group)

    for d in range(DIRS):
        vh, vl = split(to_local_ref[d])
        th, tl = split(sums[d])
        both = mm_nt(vh, jnp.concatenate([th, tl], axis=0))
        result = result + (both[:, :128] + (both[:, 128:] + mm_nt(vl, th)))
    out_ref[...] = result * valid


def local(
    multipole6,
    local5,
    box_ids,
    box_count,
    up_shift,
    down_shift,
    periodic_lattice_operator,
    multipole_to_wave_maps,
    wave_to_local_maps,
    wave_shift,
    local_source,
    local_target,
    local_class,
    remote_source,
    remote_class,
    remote_count,
    arrival_slot,
    comm=True,
):
    dma = pltpu.SemaphoreType.DMA
    operands = (
        multipole6,
        jnp.transpose(local5),
        box_ids,
        box_count,
        jnp.transpose(up_shift, (1, 0, 2)).reshape(8 * K, K),
        jnp.transpose(down_shift, (1, 0, 2)).reshape(8 * K, K),
        periodic_lattice_operator,
        multipole_to_wave_maps,
        wave_to_local_maps,
        wave_shift,
        local_source.reshape(DIRS, BLOCKS, 128),
        local_target.reshape(DIRS, BLOCKS, 128),
        local_class.reshape(DIRS, BLOCKS, 128),
        remote_source.reshape(DIRS, NEIGH, CAP),
        remote_class.reshape(DIRS, NEIGH, CAP),
        remote_count,
        arrival_slot.reshape(DIRS, NEIGH, CAP),
    )
    held = []
    for name, value in zip(LOADS, operands):
        space = pltpu.SMEM if name in ("ids", "count", "far_count") else pltpu.VMEM
        shape = (8 * KP, K) if name in ("up", "down") else value.shape
        held.append(space(shape, value.dtype))
    return pl.pallas_call(
        functools.partial(kernel, comm),
        out_shape=jax.ShapeDtypeStruct((K, SLOTS), F32),
        in_specs=[pl.BlockSpec(memory_space=pltpu.HBM)] * len(operands),
        out_specs=pl.BlockSpec(memory_space=pltpu.VMEM),
        scratch_shapes=held + [
            dma((len(operands),)),
            pltpu.VMEM((KP, 128), F32),
            pltpu.VMEM((NEIGH, KP, 128), F32),
            pltpu.VMEM((NEIGH, 8, 128), jnp.int32),
            pltpu.VMEM((NEIGH, 8, 128), jnp.int32),
            pltpu.VMEM((KP, KP), F32),
            pltpu.VMEM((8, KP, KP), BF16),
            pltpu.VMEM((8, KP, KP), BF16),
            pltpu.VMEM((8, KP, KP), BF16),
            pltpu.VMEM((8, KP, KP), BF16),
            pltpu.VMEM((DIRS, NEXP, 128), F32),
            pltpu.VMEM((NEXP, KP), F32),
            pltpu.VMEM((DIRS, NEXP, 2 * KP), BF16),
            pltpu.VMEM((BLOCKS, NEXP, 256), BF16),
            pltpu.VMEM((128, NEXP), F32),
            pltpu.VMEM((DIRS, NEXP, 128), BF16),
            pltpu.VMEM((DIRS, 128, NEXP), F32),
            pltpu.VMEM((16, 1, 128), F32),
            pltpu.VMEM((16, 1, 128), F32),
            dma((NEIGH,)),
            dma((NEIGH,)),
            dma((NEIGH,)),
            dma((NEIGH,)),
            dma((15,)),
            dma((15,)),
            dma((15,)),
            dma((15,)),
        ],
        compiler_params=pltpu.CompilerParams(
            vmem_limit_bytes=60 * 1024 * 1024,
            **(dict(collective_id=0, has_side_effects=True) if comm else {}),
        ),
        name="downward_pass",
    )(*operands)


def solution(mesh):
    split_axes = ("oct", "box")
    return jax.shard_map(
        local,
        mesh=mesh,
        in_specs=(
            P(None, split_axes),
            P(None, split_axes),
            P(split_axes),
            P(split_axes),
            P(),
            P(),
            P(),
            P(),
            P(),
            P(),
            P(None, split_axes, None),
            P(None, split_axes, None),
            P(None, split_axes, None),
            P(None, split_axes, None, None),
            P(None, split_axes, None, None),
            P(None, split_axes, None),
            P(None, split_axes, None, None),
        ),
        out_specs=P(None, split_axes),
        check_vma=False,
    )
```

```python
import functools

import jax
import jax.numpy as jnp
from jax import lax
from jax.experimental import pallas as pl
from jax.experimental.pallas import tpu as pltpu
from jax.sharding import PartitionSpec as P

K = 121
KP = 128
NEXP = 256
CLASSES = 36
DEPTH = 5
NEIGH = 8
BOX5 = 16
CAP = 64
LOC = 2048
SLOTS = 128
BLOCKS = LOC // 128
DIRS = 6
OFFSETS = [(n // 2 + 1) * (1 if n % 2 == 0 else -1) for n in range(NEIGH)]
MESH = pl.DeviceIdType.MESH
LOADS = (
    "multipole",
    "local5",
    "ids",
    "count",
    "up",
    "down",
    "lattice",
    "to_wave",
    "to_local",
    "shift",
    "near_source",
    "near_target",
    "near_class",
    "far_source",
    "far_class",
    "far_count",
    "arrival",
)
LOAD_ORDER = (
    "count",
    "far_count",
    "ids",
    "multipole",
    "far_source",
    "far_class",
    "up",
    "to_wave",
    "shift",
    "near_source",
    "near_class",
    "near_target",
    "down",
    "lattice",
    "local5",
    "arrival",
    "to_local",
)
F32 = jnp.float32
BF16 = jnp.bfloat16


def split(x):
    hi = x.astype(BF16)
    return hi, (x - hi.astype(F32)).astype(BF16)


def mm(a, b):
    return jnp.dot(a, b, preferred_element_type=F32)


def mm_nt(a, b):
    return lax.dot_general(a, b, (((1,), (1,)), ((), ())), preferred_element_type=F32)


def mm3(a, b):
    ah, al = split(a)
    bh, bl = split(b)
    return mm(ah, bh) + (mm(ah, bl) + mm(al, bh))


def pick_lanes(table, index):
    index = jnp.broadcast_to(index, table.shape)
    numbers = lax.GatherDimensionNumbers(
        offset_dims=(),
        collapsed_slice_dims=(1,),
        start_index_map=(1,),
        operand_batching_dims=(0,),
        start_indices_batching_dims=(0,),
    )
    return lax.gather(
        table,
        index[..., None],
        numbers,
        slice_sizes=(1, 1),
        mode=lax.GatherScatterMode.PROMISE_IN_BOUNDS,
    )


def lane_iota(rows):
    return lax.broadcasted_iota(jnp.int32, (rows, 128), 1)


def one_hot_rows(index):
    rows = lax.broadcasted_iota(jnp.int32, (128, 128), 0)
    return jnp.where(rows == index, 1.0, 0.0).astype(BF16)


def shift_level(high_ref, low_ref, fields, digits, operators):
    fh, fl = split(fields)
    total = jnp.zeros((KP, 128), F32)
    for at in range(0, len(operators), 2):
        group = operators[at : at + 2]
        masks = [jnp.where(digits == c, 1.0, 0.0).astype(BF16) for c in group]
        high = jnp.concatenate([high_ref[c] for c in group], axis=1)
        low = jnp.concatenate([low_ref[c] for c in group], axis=1)
        bh = jnp.concatenate([fh * mask for mask in masks], axis=0)
        bl = jnp.concatenate([fl * mask for mask in masks], axis=0)
        both = mm(high, jnp.concatenate([bh, bl], axis=1))
        total = total + (both[:, :128] + (both[:, 128:] + mm(low, bh)))
    return total


def class_factors(table, klass):
    width = klass.shape[1]
    rows = lax.broadcasted_iota(jnp.int32, (128, width), 0)
    return mm(table, jnp.where(rows % 64 == klass, 1.0, 0.0).astype(BF16))


def halves(rows):
    hi, lo = split(rows)
    return jnp.concatenate([hi, lo], axis=1)


def scatter(target, pair):
    hot = one_hot_rows(target)
    return mm_nt(jnp.concatenate([hot, hot], axis=1), pair)


def kernel(comm, *refs):
    given, out_ref, held, rest = refs[:17], refs[17], refs[18:35], refs[35:]
    (
        multipole_ref,
        local5_ref,
        ids_ref,
        count_ref,
        up_ref,
        down_ref,
        lattice_ref,
        to_wave_ref,
        to_local_ref,
        shift_ref,
        near_source_ref,
        near_target_ref,
        near_class_ref,
        far_source_ref,
        far_class_ref,
        far_count_ref,
        arrival_ref,
    ) = held
    (
        load_sem,
        moments,
        far_moments,
        pack,
        far_pack,
        padded,
        up_high,
        up_low,
        down_high,
        down_low,
        expansion,
        wide,
        wave_halves,
        held_rows,
        table_rows,
        factor,
        sums,
        ring_a,
        ring_b,
        far_send,
        far_recv,
        pack_send,
        pack_recv,
        a_send,
        a_recv,
        b_send,
        b_recv,
    ) = rest
    loads = {
        name: pltpu.make_async_copy(
            given[i],
            held[i].at[pl.ds(0, 8 * K)] if name in ("up", "down") else held[i],
            load_sem.at[i],
        )
        for i, name in enumerate(LOADS)
    }
    for name in LOAD_ORDER:
        loads[name].start()

    def loaded(*names):
        for name in names:
            loads[name].wait()

    far_moments[:, K:, :] = jnp.zeros((NEIGH, KP - K, 128), F32)

    if comm:
        octant, box = lax.axis_index("oct"), lax.axis_index("box")
        flat = octant * 32 + box
        x, core = lax.div(octant, 2), lax.rem(octant, 2)
        y, z = lax.div(box, 8), lax.rem(box, 8)

        def neighbour(offset):
            other = lax.rem(flat + offset + 256, 256)
            return lax.div(other, 32), lax.rem(other, 32)

        def peer_a(k):
            rank = lax.rem(core * 8 + z + k, 16)
            return x * 2 + lax.div(rank, 8), y * 8 + lax.rem(rank, 8)

        def peer_b(k):
            rank = lax.rem(x * 4 + y + k, 16)
            return lax.div(rank, 4) * 2 + core, lax.rem(rank, 4) * 8 + z

        barrier = pltpu.get_barrier_semaphore()
        for n in range(NEIGH):
            pl.semaphore_signal(barrier, inc=1, device_id=neighbour(OFFSETS[n]), device_id_type=MESH)

        def greet(k, carry):
            pl.semaphore_signal(barrier, inc=1, device_id=peer_a(k), device_id_type=MESH)
            pl.semaphore_signal(barrier, inc=1, device_id=peer_b(k), device_id_type=MESH)
            return carry

        lax.fori_loop(1, 16, greet, 0)

    loaded("count", "multipole")
    lanes = lane_iota(1)
    count = count_ref[0]
    valid = jnp.where(lanes < 8 * count, 1.0, 0.0)

    moments[...] = jnp.zeros((KP, 128), F32)
    moments[:K, :] = multipole_ref[...] * valid

    loaded("far_count", "far_source", "far_class")
    wide_lane = lax.broadcasted_iota(jnp.int32, (NEIGH, CAP), 1)
    row_number = lax.broadcasted_iota(jnp.int32, (NEIGH, CAP), 0)
    for d in range(DIRS):
        limit = jnp.zeros((NEIGH, CAP), jnp.int32)
        for n in range(NEIGH):
            limit = jnp.where(row_number == n, far_count_ref[d, 0, n], limit)
        source = jnp.where(wide_lane < limit, far_source_ref[d], -1)
        pack[:, d, :] = jnp.concatenate([source, far_class_ref[d]], axis=1)

    if comm:
        pl.semaphore_wait(barrier, NEIGH + 15 + 15)

        def far_copies(n):
            who = neighbour(OFFSETS[n])
            relayed = n % 4 >= 2
            near_by = neighbour(OFFSETS[n % 2]) if relayed else who
            return (
                pltpu.make_async_remote_copy(
                    src_ref=(far_moments.at[n - 2] if relayed else moments).at[pl.ds(0, K)],
                    dst_ref=far_moments.at[n, pl.ds(0, K)],
                    send_sem=far_send.at[n],
                    recv_sem=far_recv.at[n],
                    device_id=near_by,
                    device_id_type=MESH,
                ),
                pltpu.make_async_remote_copy(
                    src_ref=pack.at[n],
                    dst_ref=far_pack.at[n],
                    send_sem=pack_send.at[n],
                    recv_sem=pack_recv.at[n],
                    device_id=who,
                    device_id_type=MESH,
                ),
            )

        def sum_copy(k, ring, send, recv, peer):
            return pltpu.make_async_remote_copy(
                src_ref=ring.at[0],
                dst_ref=ring.at[k],
                send_sem=send.at[k - 1],
                recv_sem=recv.at[k - 1],
                device_id=peer(k),
                device_id_type=MESH,
            )

        def for_peers(action):
            def body(k, carry):
                action(k)
                return carry

            lax.fori_loop(1, 16, body, 0)

        copy_a = lambda k: sum_copy(k, ring_a, a_send, a_recv, peer_a)
        copy_b = lambda k: sum_copy(k, ring_b, b_send, b_recv, peer_b)
        far = [far_copies(n) for n in range(NEIGH)]
        for n in (4, 5, 0, 1):
            far[n][0].start()
        for n in range(NEIGH):
            far[n][1].start()
    else:
        for n in range(NEIGH):
            far_moments[n] = moments[...]
            far_pack[n] = pack[n]

    loaded("up", "ids")
    padded[...] = jnp.zeros((KP, KP), F32)

    def halve_operators(operators_ref, high_ref, low_ref):
        operators_ref[8 * K :, :] = jnp.zeros((8 * (KP - K), K), F32)
        for c in range(8):
            padded[:, :K] = operators_ref[pl.ds(c, KP, stride=8), :]
            high_ref[c], low_ref[c] = split(padded[...])

    halve_operators(up_ref, up_high, up_low)

    first = ids_ref[0]
    parent_of = lanes // 8
    child = lanes % 8
    ids = first + parent_of
    digit = [(ids >> (3 * (DEPTH - j))) & 7 for j in range(1, DEPTH + 1)]
    chosen = [
        [((first >> (3 * (DEPTH - j))) + i) & 7 for i in range(2 if j < DEPTH - 1 else 3)]
        for j in range(1, DEPTH)
    ] + [list(range(8))]

    upward = shift_level(up_high, up_low, moments[...], child, range(8))
    for j in range(DEPTH - 1, -1, -1):
        upward = shift_level(up_high, up_low, upward, digit[j], chosen[j])
    upward = upward * valid
    ring_a[0] = jnp.sum(jnp.transpose(upward), axis=0, keepdims=True)
    if comm:
        for_peers(lambda k: copy_a(k).start())
    loaded("to_wave", "shift", "near_source", "near_class", "near_target")

    table_rows[...] = jnp.zeros((128, NEXP), F32)
    wide[...] = jnp.zeros((NEXP, KP), F32)
    mh, ml = split(moments[...])
    for d in range(DIRS):
        wide[:, :K] = to_wave_ref[d]
        wh, wl = split(wide[...])
        wave_halves[d] = jnp.concatenate([wh, wl], axis=1)
        both = mm(wh, jnp.concatenate([mh, ml], axis=1))
        expansion[d] = both[:, :128] + (both[:, 128:] + mm(wl, mh))
        high, low = split(shift_ref[d])
        table_rows[:CLASSES, :] = high.astype(F32)
        table_rows[64 : 64 + CLASSES, :] = low.astype(F32)
        factor[d] = jnp.transpose(table_rows[...]).astype(BF16)

    def near_rows(d, block):
        klass = [near_class_ref[d, pl.ds(block + i, 1), :] for i in range(2)]
        factors = class_factors(factor[d], jnp.concatenate(klass, axis=1))
        for i in range(2):
            source = near_source_ref[d, pl.ds(block + i, 1), :]
            rows = pick_lanes(expansion[d], source) * factors[:, 128 * i : 128 * (i + 1)]
            held_rows[block + i] = halves(rows)

    def near_sums(d, block):
        return scatter(near_target_ref[d, pl.ds(block, 1), :], held_rows[block]) + scatter(
            near_target_ref[d, pl.ds(block + 1, 1), :], held_rows[block + 1]
        )

    def near_step(d, carry):
        total = jnp.zeros((128, NEXP), F32)
        for block in range(0, BLOCKS, 2):
            total = total + near_sums(d - 1, block)
            near_rows(d, block)
        sums[d - 1] = total
        return carry

    for block in range(0, BLOCKS, 2):
        near_rows(0, block)


    def hand_on(*slots):
        for n in slots:
            far[n][0].wait()
            far[n + 2][0].start()

    lax.fori_loop(1, 4, near_step, 0)
    if comm:
        hand_on(0, 1)
    lax.fori_loop(4, 5, near_step, 0)
    if comm:
        hand_on(4, 5)
        for_peers(lambda k: copy_a(k).wait())
        ring_b[0] = jnp.sum(ring_a[...], axis=0)
        for_peers(lambda k: copy_b(k).start())
    else:
        ring_b[0] = ring_a[0]

    loaded("down", "lattice", "local5", "arrival", "to_local")
    near_step(DIRS - 1, 0)
    total = jnp.zeros((128, NEXP), F32)
    for block in range(0, BLOCKS, 2):
        total = total + near_sums(DIRS - 1, block)
    sums[DIRS - 1] = total
    halve_operators(down_ref, down_high, down_low)

    first_half = lanes < CAP

    def far_blocks(group):
        for d in range(DIRS):
            sources, klasses, targets, picked = [], [], [], []
            arrival = jnp.concatenate([arrival_ref[d], arrival_ref[d]], axis=1)
            for p in (group, group + 2):
                one = far_pack[2 * p, d : d + 1, :]
                two = far_pack[2 * p + 1, d : d + 1, :]
                source = jnp.where(first_half, one, pltpu.roll(two, CAP, 1))
                klasses.append(jnp.where(first_half, pltpu.roll(one, CAP, 1), two))
                target = jnp.where(
                    first_half, arrival[2 * p : 2 * p + 1], arrival[2 * p + 1 : 2 * p + 2]
                )
                targets.append(jnp.where(source >= 0, target, -1))
                source = jnp.maximum(source, 0)
                picked.append(
                    jnp.where(
                        first_half,
                        pick_lanes(far_moments[2 * p], source),
                        pick_lanes(far_moments[2 * p + 1], source),
                    )
                )
            ph, pl_ = split(jnp.concatenate(picked, axis=1))
            both = wave_halves[d]
            rows = mm(both, jnp.concatenate([ph, ph], axis=0)) + mm(both[:, :KP], pl_)
            rows = rows * class_factors(factor[d], jnp.concatenate(klasses, axis=1))
            total = sums[d]
            for i in range(2):
                total = total + scatter(targets[i], halves(rows[:, 128 * i : 128 * (i + 1)]))
            sums[d] = total

    if comm:
        for n in (0, 1, 4, 5):
            far[n][1].wait()
    far_blocks(0)

    if comm:
        for_peers(lambda k: copy_b(k).wait())
        root = jnp.sum(ring_b[...], axis=0)
        for n in (2, 3, 6, 7):
            far[n][0].wait()
            far[n][1].wait()
    else:
        root = ring_b[0]
    padded[:K, :K] = lattice_ref[...]
    ah, al = split(padded[...])
    rh, rl = split(jnp.broadcast_to(root, (128, KP)))
    downward = mm_nt(ah, rh) + (mm_nt(ah, rl) + mm_nt(al, rh))
    for j in range(DEPTH):
        downward = shift_level(down_high, down_low, downward, digit[j], chosen[j])
    padded[...] = jnp.zeros((KP, KP), F32)
    padded[:BOX5, :K] = local5_ref[...]
    coarse = pick_lanes(jnp.transpose(padded[...]), parent_of) + downward
    result = shift_level(down_high, down_low, coarse, child, range(8))[:K]

    far_blocks(1)
    for d in range(DIRS):
        vh, vl = split(to_local_ref[d])
        th, tl = split(sums[d])
        both = mm_nt(vh, jnp.concatenate([th, tl], axis=0))
        result = result + (both[:, :128] + (both[:, 128:] + mm_nt(vl, th)))
    out_ref[...] = result


def local(
    multipole6,
    local5,
    box_ids,
    box_count,
    up_shift,
    down_shift,
    periodic_lattice_operator,
    multipole_to_wave_maps,
    wave_to_local_maps,
    wave_shift,
    local_source,
    local_target,
    local_class,
    remote_source,
    remote_class,
    remote_count,
    arrival_slot,
    comm=True,
):
    dma = pltpu.SemaphoreType.DMA
    operands = (
        multipole6,
        jnp.transpose(local5),
        box_ids,
        box_count,
        jnp.transpose(up_shift, (1, 0, 2)).reshape(8 * K, K),
        jnp.transpose(down_shift, (1, 0, 2)).reshape(8 * K, K),
        periodic_lattice_operator,
        multipole_to_wave_maps,
        wave_to_local_maps,
        wave_shift,
        local_source.reshape(DIRS, BLOCKS, 128),
        local_target.reshape(DIRS, BLOCKS, 128),
        local_class.reshape(DIRS, BLOCKS, 128),
        remote_source.reshape(DIRS, NEIGH, CAP),
        remote_class.reshape(DIRS, NEIGH, CAP),
        remote_count,
        arrival_slot.reshape(DIRS, NEIGH, CAP),
    )
    held = []
    for name, value in zip(LOADS, operands):
        space = pltpu.SMEM if name in ("ids", "count", "far_count") else pltpu.VMEM
        shape = (8 * KP, K) if name in ("up", "down") else value.shape
        held.append(space(shape, value.dtype))
    result = pl.pallas_call(
        functools.partial(kernel, comm),
        out_shape=jax.ShapeDtypeStruct((K, SLOTS), F32),
        in_specs=[pl.BlockSpec(memory_space=pltpu.HBM)] * len(operands),
        out_specs=pl.BlockSpec(memory_space=pltpu.VMEM),
        scratch_shapes=held + [
            dma((len(operands),)),
            pltpu.VMEM((KP, 128), F32),
            pltpu.VMEM((NEIGH, KP, 128), F32),
            pltpu.VMEM((NEIGH, 8, 128), jnp.int32),
            pltpu.VMEM((NEIGH, 8, 128), jnp.int32),
            pltpu.VMEM((KP, KP), F32),
            pltpu.VMEM((8, KP, KP), BF16),
            pltpu.VMEM((8, KP, KP), BF16),
            pltpu.VMEM((8, KP, KP), BF16),
            pltpu.VMEM((8, KP, KP), BF16),
            pltpu.VMEM((DIRS, NEXP, 128), F32),
            pltpu.VMEM((NEXP, KP), F32),
            pltpu.VMEM((DIRS, NEXP, 2 * KP), BF16),
            pltpu.VMEM((BLOCKS, NEXP, 256), BF16),
            pltpu.VMEM((128, NEXP), F32),
            pltpu.VMEM((DIRS, NEXP, 128), BF16),
            pltpu.VMEM((DIRS, 128, NEXP), F32),
            pltpu.VMEM((16, 1, 128), F32),
            pltpu.VMEM((16, 1, 128), F32),
            dma((NEIGH,)),
            dma((NEIGH,)),
            dma((NEIGH,)),
            dma((NEIGH,)),
            dma((15,)),
            dma((15,)),
            dma((15,)),
            dma((15,)),
        ],
        compiler_params=pltpu.CompilerParams(
            vmem_limit_bytes=60 * 1024 * 1024,
            **(dict(collective_id=0, has_side_effects=True) if comm else {}),
        ),
        name="downward_pass",
    )(*operands)
    return result * (jnp.arange(SLOTS, dtype=jnp.int32) < 8 * box_count).astype(F32)[None, :]


def solution(mesh):
    split_axes = ("oct", "box")
    return jax.shard_map(
        local,
        mesh=mesh,
        in_specs=(
            P(None, split_axes),
            P(None, split_axes),
            P(split_axes),
            P(split_axes),
            P(),
            P(),
            P(),
            P(),
            P(),
            P(),
            P(None, split_axes, None),
            P(None, split_axes, None),
            P(None, split_axes, None),
            P(None, split_axes, None, None),
            P(None, split_axes, None, None),
            P(None, split_axes, None),
            P(None, split_axes, None, None),
        ),
        out_specs=P(None, split_axes),
        check_vma=False,
    )
```
